512 devices in a mesh: dp: 64 (over y_hi, z, core), layer: 8 (over x, y_lo).
Axes of the slice: x: 4, y: 4 (y_hi: 2, y_lo: 2; y = y_hi * 2 + y_lo), z: 16, core: 2. Of those that a mesh axis runs over, the one named last changes fastest.
Arguments:
- query_inputs: bfloat16 [8, 64, 128, 4096], P('layer', 'dp'), may hold values from -6 to 6
- query_cotangents: bfloat16 [8, 64, 128, 4096], P('layer', 'dp'), may hold values from -6 to 6
- query_lengths: int32 [64], P('dp'), may hold values from 64 to 128, as said below
- proj_in: bfloat16 [8, 64, 4096], P('layer'), may hold values from -0.09375 to 0.09375
- proj_out: bfloat16 [8, 64, 4096], P('layer'), may hold values from -0.09375 to 0.09375
- out_factor: float32 [8, 64, 64], P('layer'), may hold values from -1 to 5, as said below
- in_factor: float32 [8, 64, 64], P('layer'), may hold values from -1 to 5, as said below
- train_grads: bfloat16 [8, 8192, 4096], P('layer', 'dp'), may hold values from -0.0009765625 to 0.0009765625
Outputs:
- scores: float32 [64, 8192], P('layer', 'dp')
The draws below stay inside these ranges and needn't reach their ends.
Inputs may be any that keep to these rules, and one draw needn't show every extreme that they name: `query_lengths`: some query sequence has 128 valid tokens and some has 64. `out_factor`: each matrix is symmetric positive definite. `in_factor`: each matrix is symmetric positive definite.
All inputs are finite; a program needn't handle non-finite values.
Results may differ from the reference program's by a relative error of at most 0.0057.
Values may be sent and summed in bfloat16 or wider, within the bound.
No kernel may reach another device: no remote copies, remote signals or barrier semaphores. Data moves between devices by JAX's collectives and lax.ppermute only.
A program may use at most 64 MiB of HBM per device.

```python
import math
import jax
import jax.numpy as jnp
from jax import lax

D = 4096
RANK = 64
LEN = 128
BLOCKS = 8
QUERIES = 64
TRAIN_SEQUENCES = 8192


def draw_query_lengths(key, part):
    key = jax.random.fold_in(key, 5)
    drawn = jax.random.randint(key, (QUERIES,), LEN // 2, LEN + 1, dtype=jnp.int32)
    slots = jnp.arange(QUERIES, dtype=jnp.int32)
    drawn = jnp.where(slots == 0, LEN, drawn)
    return jnp.where(slots == 1, LEN // 2, drawn)


def factor_matrix(key):
    first_key, second_key = jax.random.split(key)
    noise_draw = jax.random.normal(first_key, (BLOCKS, RANK, RANK), jnp.float32)
    symmetric = (noise_draw + jnp.swapaxes(noise_draw, 1, 2)) * (0.25 / math.sqrt(RANK))
    diagonal_entries = jnp.exp(jax.random.uniform(second_key, (BLOCKS, RANK), jnp.float32, 0.0, math.log(4.0)))
    return symmetric + jnp.eye(RANK, dtype=jnp.float32)[None, :, :] * diagonal_entries[:, None, :]


def draw_out_factor(key, part):
    key = jax.random.fold_in(key, 7)
    return factor_matrix(key)


def draw_in_factor(key, part):
    key = jax.random.fold_in(key, 11)
    return factor_matrix(key)


def block_levels(stream_key, shape, cuts, smallest, largest):
    def one(axis_at, parts):
        steps = jax.random.uniform(jax.random.fold_in(jax.random.fold_in(stream_key, 6), axis_at), (parts,), jnp.float32, smallest / len(cuts), largest / len(cuts))
        return jnp.repeat(jnp.exp(steps), shape[axis_at] // parts).reshape((-1,) + (1,) * (len(shape) - axis_at - 1))

    loudness = one(*cuts[0])
    for cut in cuts[1:]:
        loudness = loudness * one(*cut)
    return loudness


def bell_draw(own_key, extent, spread, most, pieces=(), held_as=jnp.bfloat16):
    values = spread * jax.random.normal(own_key, extent, jnp.float32)
    if pieces:
        values = values * block_levels(own_key, extent, pieces, -0.22, 0.18)
    return jnp.clip(values, -most, most).astype(held_as)


def setup_inputs(seed: int = 0) -> dict:
    key_of = jax.random.split(jax.random.key(seed), 9)
    return {
        "query_inputs": bell_draw(key_of[0], (BLOCKS, QUERIES, LEN, D), 1.0, 6.0, ((0, 8), (1, 64))),
        "query_cotangents": bell_draw(key_of[1], (BLOCKS, QUERIES, LEN, D), 1.0, 6.0, ((0, 8), (1, 64))),
        "query_lengths": draw_query_lengths(jax.random.fold_in(key_of[8], 71), 0),
        "proj_in": bell_draw(key_of[3], (BLOCKS, RANK, D), D ** -0.5, 0.09375, ((0, 8),)),
        "proj_out": bell_draw(key_of[4], (BLOCKS, RANK, D), D ** -0.5, 0.09375, ((0, 8),)),
        "out_factor": draw_out_factor(jax.random.fold_in(key_of[8], 71), 0),
        "in_factor": draw_in_factor(jax.random.fold_in(key_of[8], 71), 0),
        "train_grads": bell_draw(key_of[7], (BLOCKS, TRAIN_SEQUENCES, RANK * RANK), (RANK * RANK * LEN * 64) ** -0.5, 0.0009765625, ((0, 8), (1, 64))),
    }


def reference(query_inputs, query_cotangents, query_lengths, proj_in, proj_out, out_factor, in_factor, train_grads):
    slots = jnp.arange(LEN, dtype=jnp.int32)
    valid = slots[None, :] < query_lengths[:, None]

    def one_block(operands):
        inputs, output_cotangents, side_in, side_out, left_kronecker, right_factor, logged = operands
        out_side = jnp.einsum("qld,rd->qlr", output_cotangents.astype(jnp.float32), side_out.astype(jnp.float32))
        out_side = jnp.where(valid[:, :, None], out_side, 0.0).astype(jnp.bfloat16)
        in_side = jnp.einsum("qld,rd->qlr", inputs.astype(jnp.float32), side_in.astype(jnp.float32)).astype(jnp.bfloat16)
        query_gradient_rows = jnp.einsum("qlr,qls->qrs", out_side.astype(jnp.float32), in_side.astype(jnp.float32)).astype(jnp.bfloat16)
        left_projection = jnp.einsum("ye,dei->dyi", left_kronecker, query_gradient_rows.astype(jnp.float32), precision=lax.Precision.HIGHEST)
        both_sides = jnp.einsum("qrs,st->qrt", left_projection, right_factor, precision=lax.Precision.HIGHEST)
        conditioned = both_sides.astype(jnp.bfloat16).reshape(QUERIES, RANK * RANK)
        return jnp.dot(conditioned, logged.T, preferred_element_type=jnp.float32)

    partials = lax.map(one_block, (query_inputs, query_cotangents, proj_in, proj_out, out_factor, in_factor, train_grads))
    return jnp.sum(partials, axis=0)
```

```python
import jax
import jax.numpy as jnp
from jax import lax
from jax.sharding import Mesh, PartitionSpec as P

CORES = 2
Y_HI = 2
Y_LO = 2


def body(
    query_inputs,
    query_cotangents,
    query_lengths,
    proj_in,
    proj_out,
    out_factor,
    in_factor,
    train_grads,
):
    length = query_inputs.shape[2]
    rank = proj_in.shape[1]
    flat = rank * rank
    slots = lax.broadcasted_iota(jnp.int32, (length, 1), 0)
    out_side = jnp.einsum(
        "ld,rd->lr", query_cotangents[0, 0], proj_out[0], preferred_element_type=jnp.float32
    )
    out_side = jnp.where(slots < query_lengths[0], out_side, 0.0).astype(jnp.bfloat16)
    in_side = jnp.einsum(
        "ld,rd->lr", query_inputs[0, 0], proj_in[0], preferred_element_type=jnp.float32
    ).astype(jnp.bfloat16)
    grad = jnp.einsum("lr,ls->rs", out_side, in_side, preferred_element_type=jnp.float32)
    grad = grad.astype(jnp.bfloat16).astype(jnp.float32)
    left = jnp.dot(out_factor[0], grad, precision=lax.Precision.HIGHEST)
    conditioned = jnp.dot(left, in_factor[0], precision=lax.Precision.HIGHEST)
    conditioned = conditioned.astype(jnp.bfloat16).reshape(flat // 128, 128)

    places = lax.axis_size(("yh", "z"))
    sent = jnp.broadcast_to(conditioned[None], (places, flat // 128, 128))
    mine = lax.all_to_all(sent, ("yh", "z"), 0, 0)
    swap = [(i, CORES - 1 - i) for i in range(CORES)]
    other = lax.ppermute(mine, "core", swap)
    first = lax.axis_index("core") == 0
    even = jnp.where(first, mine, other)
    odd = jnp.where(first, other, mine)
    queries = jnp.stack([even, odd], axis=1).reshape(places * CORES, flat)

    partial = lax.dot_general(
        queries, train_grads[0], (((1,), (1,)), ((), ())), preferred_element_type=jnp.float32
    )
    layers = lax.axis_size(("x", "yl"))
    terms = lax.all_to_all(
        partial.reshape(layers, -1, partial.shape[1]), ("x", "yl"), 0, 0
    )
    return jnp.sum(terms, axis=0)


def solution(mesh):
    dp, layer = mesh.devices.shape
    shape = (Y_HI, dp // (Y_HI * CORES), CORES, layer // Y_LO, Y_LO)
    fine = Mesh(mesh.devices.reshape(shape), ("yh", "z", "core", "x", "yl"))
    dp, layer = ("yh", "z", "core"), ("x", "yl")
    in_specs = (
        P(layer, dp, None, None),
        P(layer, dp, None, None),
        P(dp),
        P(layer, None, None),
        P(layer, None, None),
        P(layer, None, None),
        P(layer, None, None),
        P(layer, dp, None),
    )
    return jax.shard_map(
        body, mesh=fine, in_specs=in_specs, out_specs=P(layer, dp), check_vma=False
    )
```

```python
import functools
import jax
import jax.numpy as jnp
from jax import lax
from jax.experimental import pallas as pl
from jax.experimental.pallas import tpu as pltpu
from jax.sharding import Mesh, PartitionSpec as P

PIECES = 4


def _own_kernel(copies, x_hbm, c_hbm, n_ref, pi_hbm, po_hbm, a_hbm, b_hbm, o_ref, x, c, pi, po, a, b, sems):
    length, width = x.shape
    rank = pi.shape[0]
    step = width // PIECES
    started = []
    for p in range(PIECES):
        cols = pl.ds(p * step, step)
        group = [
            pltpu.make_async_copy(src.at[:, cols], dst.at[:, cols], sems.at[4 * p + i])
            for i, (src, dst) in enumerate(((c_hbm, c), (po_hbm, po), (x_hbm, x), (pi_hbm, pi)))
        ]
        for copy in group:
            copy.start()
        started.append(group)
    factors = [
        pltpu.make_async_copy(a_hbm, a, sems.at[4 * PIECES]),
        pltpu.make_async_copy(b_hbm, b, sems.at[4 * PIECES + 1]),
    ]
    for copy in factors:
        copy.start()
    out_side = jnp.zeros((rank, length), jnp.float32)
    in_side = jnp.zeros((length, rank), jnp.float32)
    nt = (((1,), (1,)), ((), ()))
    for p in range(PIECES):
        cols = pl.ds(p * step, step)
        group = started[p]
        group[0].wait()
        group[1].wait()
        out_side += lax.dot_general(po[:, cols], c[:, cols], nt, preferred_element_type=jnp.float32)
        group[2].wait()
        group[3].wait()
        in_side += lax.dot_general(x[:, cols], pi[:, cols], nt, preferred_element_type=jnp.float32)
    slots = lax.broadcasted_iota(jnp.int32, (rank, length), 1)
    out_side = jnp.where(slots < n_ref[0], out_side, 0.0).astype(jnp.bfloat16)
    grad = jnp.dot(out_side, in_side.astype(jnp.bfloat16), preferred_element_type=jnp.float32)
    grad = grad.astype(jnp.bfloat16).astype(jnp.float32)
    for copy in factors:
        copy.wait()
    half = rank // 2
    rows = jnp.concatenate([a[pl.ds(0, half, stride=2), :], a[pl.ds(1, half, stride=2), :]], axis=0)
    left = jnp.dot(rows, grad, precision=lax.Precision.HIGHEST, preferred_element_type=jnp.float32)
    both = jnp.dot(left, b[...], precision=lax.Precision.HIGHEST, preferred_element_type=jnp.float32)
    paired = jnp.concatenate([both[:half], both[half:]], axis=1).astype(jnp.bfloat16)
    for i in range(copies):
        o_ref[i] = paired


def own_gradient(copies, x, c, n, pi, po, a, b):
    length, width = x.shape
    rank = pi.shape[0]
    any_ = pl.BlockSpec(memory_space=pltpu.HBM)
    return pl.pallas_call(
        functools.partial(_own_kernel, copies),
        out_shape=jax.ShapeDtypeStruct((copies, rank // 2, 2 * rank), jnp.bfloat16),
        in_specs=[any_, any_, pl.BlockSpec(memory_space=pltpu.SMEM), any_, any_, any_, any_],
        out_specs=pl.BlockSpec(memory_space=pltpu.VMEM),
        scratch_shapes=[
            pltpu.VMEM((length, width), jnp.bfloat16),
            pltpu.VMEM((length, width), jnp.bfloat16),
            pltpu.VMEM((rank, width), jnp.bfloat16),
            pltpu.VMEM((rank, width), jnp.bfloat16),
            pltpu.VMEM((rank, rank), jnp.float32),
            pltpu.VMEM((rank, rank), jnp.float32),
            pltpu.SemaphoreType.DMA((4 * PIECES + 2,)),
        ],
        compiler_params=pltpu.CompilerParams(vmem_limit_bytes=56 * 1024 * 1024),
        name="own_gradient",
    )(x, c, n, pi, po, a, b)

CORES = 2
Y_HI = 2
Y_LO = 2
Z_FIRST = 8
LAYER_FIRST = 7


def turned(count, first):
    return [[(i + first) % count for i in range(count)]]


def swapped(held, axis):
    other = lax.ppermute(held, axis, [(0, 1), (1, 0)])
    lower = lax.axis_index(axis) == 0
    return jnp.stack([jnp.where(lower, held, other), jnp.where(lower, other, held)])


def body(
    query_inputs,
    query_cotangents,
    query_lengths,
    proj_in,
    proj_out,
    out_factor,
    in_factor,
    train_grads,
):
    flat = train_grads.shape[2]
    train = train_grads.shape[1]
    places = lax.axis_size("z")
    sent = own_gradient(
        places,
        query_inputs[0, 0],
        query_cotangents[0, 0],
        query_lengths,
        proj_in[0],
        proj_out[0],
        out_factor[0],
        in_factor[0],
    )
    held = lax.all_to_all(sent, "z", 0, 0, axis_index_groups=turned(places, Z_FIRST))
    held = swapped(held, "yh")
    held = swapped(held, "core")
    queries = held.reshape(-1, flat)
    partial = lax.dot_general(
        queries, train_grads[0], (((1,), (1,)), ((), ())), preferred_element_type=jnp.float32
    )
    partial = partial.reshape(CORES, Y_HI, places, train)
    partial = jnp.roll(partial, Z_FIRST, axis=2).transpose(1, 2, 0, 3)
    layers = lax.axis_size(("x", "yl"))
    partial = partial.reshape(layers, -1, train)
    partial = jnp.roll(partial, -LAYER_FIRST, axis=0)
    terms = lax.all_to_all(
        partial, ("x", "yl"), 0, 0, axis_index_groups=turned(layers, LAYER_FIRST)
    )
    return jnp.sum(terms, axis=0)


def solution(mesh):
    dp, layer = mesh.devices.shape
    shape = (Y_HI, dp // (Y_HI * CORES), CORES, layer // Y_LO, Y_LO)
    fine = Mesh(mesh.devices.reshape(shape), ("yh", "z", "core", "x", "yl"))
    dp, layer = ("yh", "z", "core"), ("x", "yl")
    in_specs = (
        P(layer, dp, None, None),
        P(layer, dp, None, None),
        P(dp),
        P(layer, None, None),
        P(layer, None, None),
        P(layer, None, None),
        P(layer, None, None),
        P(layer, dp, None),
    )
    return jax.shard_map(
        body, mesh=fine, in_specs=in_specs, out_specs=P(layer, dp), check_vma=False
    )
```

```python
import functools
import jax
import jax.numpy as jnp
from jax import lax
from jax.experimental import pallas as pl
from jax.experimental.pallas import tpu as pltpu
from jax.sharding import Mesh, PartitionSpec as P

PIECES = 4


def _own_kernel(copies, x_hbm, c_hbm, n_ref, pi_hbm, po_hbm, a_hbm, b_hbm, o_ref, x, c, pi, po, a, b, sems):
    length, width = x.shape
    rank = pi.shape[0]
    step = width // PIECES
    started = []
    for p in range(PIECES):
        cols = pl.ds(p * step, step)
        group = [
            pltpu.make_async_copy(src.at[:, cols], dst.at[:, cols], sems.at[4 * p + i])
            for i, (src, dst) in enumerate(((c_hbm, c), (po_hbm, po), (x_hbm, x), (pi_hbm, pi)))
        ]
        for copy in group:
            copy.start()
        started.append(group)
    factors = [
        pltpu.make_async_copy(a_hbm, a, sems.at[4 * PIECES]),
        pltpu.make_async_copy(b_hbm, b, sems.at[4 * PIECES + 1]),
    ]
    for copy in factors:
        copy.start()
    out_side = jnp.zeros((rank, length), jnp.float32)
    in_side = jnp.zeros((length, rank), jnp.float32)
    nt = (((1,), (1,)), ((), ()))
    for p in range(PIECES):
        cols = pl.ds(p * step, step)
        group = started[p]
        group[0].wait()
        group[1].wait()
        out_side += lax.dot_general(po[:, cols], c[:, cols], nt, preferred_element_type=jnp.float32)
        group[2].wait()
        group[3].wait()
        in_side += lax.dot_general(x[:, cols], pi[:, cols], nt, preferred_element_type=jnp.float32)
    slots = lax.broadcasted_iota(jnp.int32, (rank, length), 1)
    out_side = jnp.where(slots < n_ref[0], out_side, 0.0).astype(jnp.bfloat16)
    grad = jnp.dot(out_side, in_side.astype(jnp.bfloat16), preferred_element_type=jnp.float32)
    grad = grad.astype(jnp.bfloat16).astype(jnp.float32)
    for copy in factors:
        copy.wait()
    half = rank // 2
    rows = jnp.concatenate([a[pl.ds(0, half, stride=2), :], a[pl.ds(1, half, stride=2), :]], axis=0)
    left = jnp.dot(rows, grad, precision=lax.Precision.HIGHEST, preferred_element_type=jnp.float32)
    both = jnp.dot(left, b[...], precision=lax.Precision.HIGHEST, preferred_element_type=jnp.float32)
    paired = jnp.concatenate([both[:half], both[half:]], axis=1).astype(jnp.bfloat16)
    for i in range(copies):
        o_ref[i] = paired


def own_gradient(copies, x, c, n, pi, po, a, b):
    length, width = x.shape
    rank = pi.shape[0]
    any_ = pl.BlockSpec(memory_space=pltpu.HBM)
    return pl.pallas_call(
        functools.partial(_own_kernel, copies),
        out_shape=jax.ShapeDtypeStruct((copies, rank // 2, 2 * rank), jnp.bfloat16),
        in_specs=[any_, any_, pl.BlockSpec(memory_space=pltpu.SMEM), any_, any_, any_, any_],
        out_specs=pl.BlockSpec(memory_space=pltpu.VMEM),
        scratch_shapes=[
            pltpu.VMEM((length, width), jnp.bfloat16),
            pltpu.VMEM((length, width), jnp.bfloat16),
            pltpu.VMEM((rank, width), jnp.bfloat16),
            pltpu.VMEM((rank, width), jnp.bfloat16),
            pltpu.VMEM((rank, rank), jnp.float32),
            pltpu.VMEM((rank, rank), jnp.float32),
            pltpu.SemaphoreType.DMA((4 * PIECES + 2,)),
        ],
        compiler_params=pltpu.CompilerParams(vmem_limit_bytes=56 * 1024 * 1024),
        name="own_gradient",
    )(x, c, n, pi, po, a, b)

CORES = 2
Y_HI = 2
Y_LO = 2
Z_FIRST = 8


def turned(count, first):
    return [[(i + first) % count for i in range(count)]]


def swapped(held, axis):
    other = lax.ppermute(held, axis, [(0, 1), (1, 0)])
    lower = lax.axis_index(axis) == 0
    return jnp.stack([jnp.where(lower, held, other), jnp.where(lower, other, held)])


def body(
    query_inputs,
    query_cotangents,
    query_lengths,
    proj_in,
    proj_out,
    out_factor,
    in_factor,
    train_grads,
):
    flat = train_grads.shape[2]
    train = train_grads.shape[1]
    places = lax.axis_size("z")
    sent = own_gradient(
        places,
        query_inputs[0, 0],
        query_cotangents[0, 0],
        query_lengths,
        proj_in[0],
        proj_out[0],
        out_factor[0],
        in_factor[0],
    )
    mine = train_grads[0]
    theirs = lax.ppermute(mine, "core", [(0, 1), (1, 0)])
    held = lax.all_to_all(sent, "z", 0, 0, axis_index_groups=turned(places, Z_FIRST))
    nt = (((1,), (1,)), ((), ()))
    layers = lax.axis_size(("x", "yl"))

    def scores(rows):
        part = lax.dot_general(queries, rows, nt, preferred_element_type=jnp.float32)
        part = part.reshape(-1, places, train)
        return jnp.roll(part, Z_FIRST, axis=1)

    queries = swapped(held, "yh").reshape(-1, flat)
    here, there = scores(mine), scores(theirs)
    lower = lax.axis_index("core") == 0
    both = jnp.stack([jnp.where(lower, here, there), jnp.where(lower, there, here)])
    both = both.reshape(CORES * layers, -1, train)
    both = jnp.roll(both, 1, axis=0)
    terms = lax.all_to_all(
        both, ("core", "x", "yl"), 0, 0, axis_index_groups=turned(CORES * layers, CORES * layers - 1)
    )
    terms = jnp.roll(terms, -1, axis=0).reshape((CORES, layers) + terms.shape[1:])
    return jnp.sum(terms, axis=1).transpose(1, 0, 2).reshape(-1, train)


def solution(mesh):
    dp, layer = mesh.devices.shape
    shape = (Y_HI, dp // (Y_HI * CORES), CORES, layer // Y_LO, Y_LO)
    fine = Mesh(mesh.devices.reshape(shape), ("yh", "z", "core", "x", "yl"))
    dp, layer = ("yh", "z", "core"), ("x", "yl")
    in_specs = (
        P(layer, dp, None, None),
        P(layer, dp, None, None),
        P(dp),
        P(layer, None, None),
        P(layer, None, None),
        P(layer, None, None),
        P(layer, None, None),
        P(layer, dp, None),
    )
    return jax.shard_map(
        body, mesh=fine, in_specs=in_specs, out_specs=P(layer, dp), check_vma=False
    )
```

```python
import functools
import jax
import jax.numpy as jnp
from jax import lax
from jax.experimental import pallas as pl
from jax.experimental.pallas import tpu as pltpu
from jax.sharding import Mesh, PartitionSpec as P

PIECES = 4


def _own_kernel(copies, x_hbm, c_hbm, n_hbm, pi_hbm, po_hbm, a_hbm, b_hbm, o_ref, x, c, n, pi, po, a, b, sems):
    length, width = x.shape
    rank = pi.shape[0]
    step = width // PIECES
    started = []
    for p in range(PIECES):
        cols = pl.ds(p * step, step)
        group = [
            pltpu.make_async_copy(src.at[:, cols], dst.at[:, cols], sems.at[4 * p + i])
            for i, (src, dst) in enumerate(((c_hbm, c), (po_hbm, po), (x_hbm, x), (pi_hbm, pi)))
        ]
        for copy in group:
            copy.start()
        started.append(group)
    factors = [
        pltpu.make_async_copy(a_hbm, a, sems.at[4 * PIECES]),
        pltpu.make_async_copy(b_hbm, b, sems.at[4 * PIECES + 1]),
        pltpu.make_async_copy(n_hbm, n, sems.at[4 * PIECES + 2]),
    ]
    for copy in factors:
        copy.start()
    out_side = jnp.zeros((rank, length), jnp.float32)
    in_side = jnp.zeros((length, rank), jnp.float32)
    nt = (((1,), (1,)), ((), ()))
    for p in range(PIECES):
        cols = pl.ds(p * step, step)
        group = started[p]
        group[0].wait()
        group[1].wait()
        out_side += lax.dot_general(po[:, cols], c[:, cols], nt, preferred_element_type=jnp.float32)
        group[2].wait()
        group[3].wait()
        in_side += lax.dot_general(x[:, cols], pi[:, cols], nt, preferred_element_type=jnp.float32)
    for copy in factors:
        copy.wait()
    slots = lax.broadcasted_iota(jnp.int32, (rank, length), 1)
    out_side = jnp.where(slots < n[0], out_side, 0.0).astype(jnp.bfloat16)
    grad = jnp.dot(out_side, in_side.astype(jnp.bfloat16), preferred_element_type=jnp.float32)
    grad = grad.astype(jnp.bfloat16).astype(jnp.float32)
    half = rank // 2
    rows = jnp.concatenate([a[pl.ds(0, half, stride=2), :], a[pl.ds(1, half, stride=2), :]], axis=0)
    left = jnp.dot(rows, grad, precision=lax.Precision.HIGHEST, preferred_element_type=jnp.float32)
    both = jnp.dot(left, b[...], precision=lax.Precision.HIGHEST, preferred_element_type=jnp.float32)
    paired = jnp.concatenate([both[:half], both[half:]], axis=1).astype(jnp.bfloat16)
    for i in range(copies):
        o_ref[i] = paired


def own_gradient(copies, x, c, n, pi, po, a, b):
    length, width = x.shape
    rank = pi.shape[0]
    any_ = pl.BlockSpec(memory_space=pl.ANY)
    return pl.pallas_call(
        functools.partial(_own_kernel, copies),
        out_shape=jax.ShapeDtypeStruct((copies, rank // 2, 2 * rank), jnp.bfloat16),
        in_specs=[any_, any_, pl.BlockSpec(memory_space=pltpu.HBM)] + [any_] * 4,
        out_specs=pl.BlockSpec(memory_space=pltpu.VMEM),
        scratch_shapes=[
            pltpu.VMEM((length, width), jnp.bfloat16),
            pltpu.VMEM((length, width), jnp.bfloat16),
            pltpu.SMEM((1,), jnp.int32),
            pltpu.VMEM((rank, width), jnp.bfloat16),
            pltpu.VMEM((rank, width), jnp.bfloat16),
            pltpu.VMEM((rank, rank), jnp.float32),
            pltpu.VMEM((rank, rank), jnp.float32),
            pltpu.SemaphoreType.DMA((4 * PIECES + 3,)),
        ],
        compiler_params=pltpu.CompilerParams(vmem_limit_bytes=16 * 1024 * 1024),
        name="own_gradient",
    )(x, c, n, pi, po, a, b)


CORES = 2
Y_HI = 2
Y_LO = 2
RUN = 4


def runs_of(places):
    half = places // RUN // 2
    return [r for i in range(half) for r in (half + i, i)]


def swap(array, axis):
    return lax.ppermute(array, axis, [(0, 1), (1, 0)])


def last_first(count):
    return [[(i + count - 1) % count for i in range(count)]]


def own_sent(query_inputs, query_cotangents, query_lengths, proj_in, proj_out, out_factor, in_factor):
    return own_gradient(
        lax.axis_size("z"),
        pltpu.with_memory_space_constraint(query_inputs[0, 0], pltpu.HBM),
        pltpu.with_memory_space_constraint(query_cotangents[0, 0], pltpu.HBM),
        query_lengths,
        pltpu.with_memory_space_constraint(proj_in[0], pltpu.HBM),
        pltpu.with_memory_space_constraint(proj_out[0], pltpu.HBM),
        pltpu.with_memory_space_constraint(out_factor[0], pltpu.HBM),
        pltpu.with_memory_space_constraint(in_factor[0], pltpu.HBM),
    )


def gathered(sent):
    places = lax.axis_size("z")
    order = [r * RUN + i for r in runs_of(places) for i in range(RUN)]
    return lax.all_to_all(sent, "z", 0, 0, axis_index_groups=[order])


def both_scores(q_ref, more_ref, mine_ref, theirs_ref):
    nt = (((1,), (1,)), ((), ()))
    q = jnp.concatenate([q_ref[...], more_ref[...]], axis=0)
    mine = lax.dot_general(q, mine_ref[...], nt, preferred_element_type=jnp.float32)
    theirs = lax.dot_general(q, theirs_ref[...], nt, preferred_element_type=jnp.float32)
    return mine, theirs


def scored(kernel, shape, queries, more, mine, theirs):
    vmem = pl.BlockSpec(memory_space=pltpu.VMEM)
    return pl.pallas_call(
        kernel,
        out_shape=jax.ShapeDtypeStruct(shape, jnp.float32),
        in_specs=[vmem] * 4,
        out_specs=vmem,
        compiler_params=pltpu.CompilerParams(vmem_limit_bytes=16 * 1024 * 1024),
        name="scored",
    )(queries, more, mine, theirs)


def _score_kernel(places, q_ref, more_ref, mine_ref, theirs_ref, o_ref):
    mine, theirs = both_scores(q_ref, more_ref, mine_ref, theirs_ref)
    core, yh = lax.axis_index("core"), lax.axis_index("yh")
    blocks = o_ref.shape[0]
    runs = runs_of(places)
    for h in range(Y_HI):
        part = jnp.where(yh == h, mine, theirs)
        first = jnp.where(core == 0, part[:places], part[places:])
        second = jnp.where(core == 0, part[places:], part[:places])
        for i, r in enumerate(runs):
            rows = slice(i * RUN, (i + 1) * RUN)
            block = jnp.concatenate([first[rows], second[rows]], axis=0)
            for half in range(Y_HI):
                o_ref[((h * Y_HI + half) * len(runs) + r + 1) % blocks] = block


def body(
    query_inputs,
    query_cotangents,
    query_lengths,
    proj_in,
    proj_out,
    out_factor,
    in_factor,
    train_grads,
):
    flat = train_grads.shape[2]
    train = train_grads.shape[1]
    places = lax.axis_size("z")
    layers = lax.axis_size(("x", "yl"))
    mine = train_grads[0]
    sent = own_sent(
        query_inputs, query_cotangents, query_lengths, proj_in, proj_out, out_factor, in_factor
    )
    ahead = mine
    theirs = swap(ahead, "yh")
    held = gathered(sent)
    held, theirs = lax.optimization_barrier((held, theirs))
    more = swap(held, "core")
    parts = scored(
        functools.partial(_score_kernel, places),
        (Y_HI * layers, CORES * RUN, train),
        held.reshape(places, flat),
        more.reshape(places, flat),
        mine,
        theirs,
    )
    asked = lax.axis_index(("x", "yl")) // (layers // Y_HI) == 0
    parts, asked = lax.optimization_barrier((parts, asked))
    terms = lax.all_to_all(
        parts, ("yh", "x", "yl"), 0, 0, axis_index_groups=last_first(Y_HI * layers)
    )
    terms = jnp.roll(terms, -1, axis=0).reshape((Y_HI, layers) + terms.shape[1:])
    terms = jnp.sum(jnp.where(asked, terms[0], terms[1]), axis=0)
    return terms.reshape(CORES, RUN, train).transpose(1, 0, 2).reshape(-1, train)


def solution(mesh):
    dp, layer = mesh.devices.shape
    shape = (Y_HI, dp // (Y_HI * CORES), CORES, layer // Y_LO, Y_LO)
    fine = Mesh(mesh.devices.reshape(shape), ("yh", "z", "core", "x", "yl"))
    dp, layer = ("yh", "z", "core"), ("x", "yl")
    in_specs = (
        P(layer, dp, None, None),
        P(layer, dp, None, None),
        P(dp),
        P(layer, None, None),
        P(layer, None, None),
        P(layer, None, None),
        P(layer, None, None),
        P(layer, dp, None),
    )
    return jax.shard_map(
        body, mesh=fine, in_specs=in_specs, out_specs=P(layer, dp), check_vma=False
    )
```

```python
import functools
import jax
import jax.numpy as jnp
from jax import lax
from jax.experimental import pallas as pl
from jax.experimental.pallas import tpu as pltpu
from jax.sharding import Mesh, PartitionSpec as P

PIECES = 4


def _own_kernel(copies, x_hbm, c_hbm, n_hbm, pi_hbm, po_hbm, a_hbm, b_hbm, o_ref, x, c, n, pi, po, a, b, sems):
    length, width = x.shape
    rank = pi.shape[0]
    step = width // PIECES
    started = []
    for p in range(PIECES):
        cols = pl.ds(p * step, step)
        group = [
            pltpu.make_async_copy(src.at[:, cols], dst.at[:, cols], sems.at[4 * p + i])
            for i, (src, dst) in enumerate(((c_hbm, c), (po_hbm, po), (x_hbm, x), (pi_hbm, pi)))
        ]
        for copy in group:
            copy.start()
        started.append(group)
    factors = [
        pltpu.make_async_copy(a_hbm, a, sems.at[4 * PIECES]),
        pltpu.make_async_copy(b_hbm, b, sems.at[4 * PIECES + 1]),
        pltpu.make_async_copy(n_hbm, n, sems.at[4 * PIECES + 2]),
    ]
    for copy in factors:
        copy.start()
    out_side = jnp.zeros((rank, length), jnp.float32)
    in_side = jnp.zeros((length, rank), jnp.float32)
    nt = (((1,), (1,)), ((), ()))
    for p in range(PIECES):
        cols = pl.ds(p * step, step)
        group = started[p]
        group[0].wait()
        group[1].wait()
        out_side += lax.dot_general(po[:, cols], c[:, cols], nt, preferred_element_type=jnp.float32)
        group[2].wait()
        group[3].wait()
        in_side += lax.dot_general(x[:, cols], pi[:, cols], nt, preferred_element_type=jnp.float32)
    for copy in factors:
        copy.wait()
    slots = lax.broadcasted_iota(jnp.int32, (rank, length), 1)
    out_side = jnp.where(slots < n[0], out_side, 0.0).astype(jnp.bfloat16)
    grad = jnp.dot(out_side, in_side.astype(jnp.bfloat16), preferred_element_type=jnp.float32)
    grad = grad.astype(jnp.bfloat16).astype(jnp.float32)
    half = rank // 2
    rows = jnp.concatenate([a[pl.ds(0, half, stride=2), :], a[pl.ds(1, half, stride=2), :]], axis=0)
    left = jnp.dot(rows, grad, precision=lax.Precision.HIGHEST, preferred_element_type=jnp.float32)
    both = jnp.dot(left, b[...], precision=lax.Precision.HIGHEST, preferred_element_type=jnp.float32)
    paired = jnp.concatenate([both[:half], both[half:]], axis=1).astype(jnp.bfloat16)
    for i in range(copies):
        o_ref[i] = paired


def own_gradient(copies, x, c, n, pi, po, a, b):
    length, width = x.shape
    rank = pi.shape[0]
    any_ = pl.BlockSpec(memory_space=pl.ANY)
    return pl.pallas_call(
        functools.partial(_own_kernel, copies),
        out_shape=jax.ShapeDtypeStruct((copies, rank // 2, 2 * rank), jnp.bfloat16),
        in_specs=[any_, any_, pl.BlockSpec(memory_space=pltpu.HBM)] + [any_] * 4,
        out_specs=pl.BlockSpec(memory_space=pltpu.VMEM),
        scratch_shapes=[
            pltpu.VMEM((length, width), jnp.bfloat16),
            pltpu.VMEM((length, width), jnp.bfloat16),
            pltpu.SMEM((1,), jnp.int32),
            pltpu.VMEM((rank, width), jnp.bfloat16),
            pltpu.VMEM((rank, width), jnp.bfloat16),
            pltpu.VMEM((rank, rank), jnp.float32),
            pltpu.VMEM((rank, rank), jnp.float32),
            pltpu.SemaphoreType.DMA((4 * PIECES + 3,)),
        ],
        compiler_params=pltpu.CompilerParams(vmem_limit_bytes=16 * 1024 * 1024),
        name="own_gradient",
    )(x, c, n, pi, po, a, b)


CORES = 2
Y_HI = 2
Y_LO = 2
RUN = 4
EARLY = 7


def runs_of(places):
    half = places // RUN // 2
    return [r for i in range(half) for r in (half + i, i)]


def pairs(planes, places):
    over_y = [(h * places + z, (1 - h) * places + z) for z in planes for h in range(Y_HI)]
    over_core = [(CORES * z + c, CORES * z + 1 - c) for z in planes for c in range(CORES)]
    return over_y, over_core


def last_first(count):
    return [[(i + count - 1) % count for i in range(count)]]


def own_sent(query_inputs, query_cotangents, query_lengths, proj_in, proj_out, out_factor, in_factor):
    return own_gradient(
        lax.axis_size("z"),
        pltpu.with_memory_space_constraint(query_inputs[0, 0], pltpu.HBM),
        pltpu.with_memory_space_constraint(query_cotangents[0, 0], pltpu.HBM),
        query_lengths,
        pltpu.with_memory_space_constraint(proj_in[0], pltpu.HBM),
        pltpu.with_memory_space_constraint(proj_out[0], pltpu.HBM),
        pltpu.with_memory_space_constraint(out_factor[0], pltpu.HBM),
        pltpu.with_memory_space_constraint(in_factor[0], pltpu.HBM),
    )


def gathered(sent):
    places = lax.axis_size("z")
    order = [r * RUN + i for r in runs_of(places) for i in range(RUN)]
    return lax.all_to_all(sent, "z", 0, 0, axis_index_groups=[order])


def _mine_kernel(q_ref, core_q_ref, yh_q_ref, mine_ref, o_ref):
    nt = (((1,), (1,)), ((), ()))
    z = lax.axis_index("z")

    def score(more_ref):
        q = jnp.concatenate([q_ref[...], more_ref[...]], axis=0)
        o_ref[...] = lax.dot_general(q, mine_ref[...], nt, preferred_element_type=jnp.float32)

    @pl.when(z < EARLY)
    def _():
        score(core_q_ref)

    @pl.when(z >= EARLY)
    def _():
        score(yh_q_ref)


def scored_mine(*operands):
    vmem = pl.BlockSpec(memory_space=pltpu.VMEM)
    rows, train = 2 * operands[0].shape[0], operands[3].shape[0]
    return pl.pallas_call(
        _mine_kernel,
        out_shape=jax.ShapeDtypeStruct((rows, train), jnp.float32),
        in_specs=[vmem] * 4,
        out_specs=vmem,
        compiler_params=pltpu.CompilerParams(vmem_limit_bytes=16 * 1024 * 1024),
        cost_estimate=pl.CostEstimate(flops=10000000000, bytes_accessed=1 << 20, transcendentals=0),
        name="scored_mine",
    )(*operands)


def _score_kernel(places, q_ref, core_q_ref, yh_q_ref, mine_s, yh_ref, core_ref, o_ref, other_s):
    nt = (((1,), (1,)), ((), ()))
    yh, core, z = lax.axis_index("yh"), lax.axis_index("core"), lax.axis_index("z")
    blocks = o_ref.shape[0]
    layers = blocks // (Y_HI * CORES)
    runs = runs_of(places)
    o_ref[...] = jnp.zeros(o_ref.shape, o_ref.dtype)

    def score(more_ref, other_ref):
        q = jnp.concatenate([q_ref[...], more_ref[...]], axis=0)
        other_s[...] = lax.dot_general(q, other_ref[...], nt, preferred_element_type=jnp.float32)

    def put(h, c, layer, first, second):
        rows = jnp.concatenate([first, second], axis=0)
        o_ref[lax.rem((h * CORES + c) * layers + layer + 1, blocks)] = rows

    @pl.when(z < EARLY)
    def _():
        score(core_q_ref, yh_ref)
        for s, h in ((mine_s, yh), (other_s, 1 - yh)):
            for i, r in enumerate(runs):
                own = s[i * RUN : (i + 1) * RUN]
                more = s[places + i * RUN : places + (i + 1) * RUN]
                first = jnp.where(core == 0, own, more)
                put(h, core, yh * len(runs) + r, first, jnp.where(core == 0, more, own))

    @pl.when(z >= EARLY)
    def _():
        score(yh_q_ref, core_ref)
        for s, c in ((mine_s, core), (other_s, 1 - core)):
            for half, h in ((0, yh), (1, 1 - yh)):
                for i, r in enumerate(runs):
                    at = half * places + i * RUN
                    own = s[at : at + RUN]
                    none = jnp.zeros_like(own)
                    put(yh, c, h * len(runs) + r, jnp.where(core == 0, own, none), jnp.where(core == 0, none, own))


def scored(places, layers, *operands):
    train = operands[3].shape[1]
    vmem = pl.BlockSpec(memory_space=pltpu.VMEM)
    return pl.pallas_call(
        functools.partial(_score_kernel, places),
        out_shape=jax.ShapeDtypeStruct((Y_HI * CORES * layers, CORES * RUN, train), jnp.float32),
        in_specs=[vmem] * 6,
        out_specs=vmem,
        scratch_shapes=[pltpu.VMEM((2 * places, train), jnp.float32)],
        compiler_params=pltpu.CompilerParams(vmem_limit_bytes=16 * 1024 * 1024),
        name="scored",
    )(*operands)


def body(
    query_inputs,
    query_cotangents,
    query_lengths,
    proj_in,
    proj_out,
    out_factor,
    in_factor,
    train_grads,
):
    flat = train_grads.shape[2]
    train = train_grads.shape[1]
    places = lax.axis_size("z")
    layers = lax.axis_size(("x", "yl"))
    mine = train_grads[0]
    early_yh, early_core = pairs(range(EARLY), places)
    late_yh, late_core = pairs(range(EARLY, places), places)
    sent = own_sent(
        query_inputs, query_cotangents, query_lengths, proj_in, proj_out, out_factor, in_factor
    )
    yh_rows = lax.ppermute(mine, ("yh", "z"), early_yh)
    held, yh_rows, after = lax.optimization_barrier((gathered(sent), yh_rows, mine))
    yh_queries = lax.ppermute(held, ("yh", "z"), late_yh)
    core_queries = lax.ppermute(held, ("z", "core"), early_core)
    core_rows = lax.ppermute(after, ("z", "core"), late_core)
    queries = [q.reshape(places, flat) for q in (held, core_queries, yh_queries)]
    parts = scored(places, layers, *queries, scored_mine(*queries, mine), yh_rows, core_rows)
    terms = lax.all_to_all(
        parts, ("yh", "core", "x", "yl"), 0, 0, axis_index_groups=last_first(parts.shape[0])
    )
    terms = jnp.sum(terms, axis=0)
    return terms.reshape(CORES, RUN, train).transpose(1, 0, 2).reshape(-1, train)


def solution(mesh):
    dp, layer = mesh.devices.shape
    shape = (Y_HI, dp // (Y_HI * CORES), CORES, layer // Y_LO, Y_LO)
    fine = Mesh(mesh.devices.reshape(shape), ("yh", "z", "core", "x", "yl"))
    dp, layer = ("yh", "z", "core"), ("x", "yl")
    in_specs = (
        P(layer, dp, None, None),
        P(layer, dp, None, None),
        P(dp),
        P(layer, None, None),
        P(layer, None, None),
        P(layer, None, None),
        P(layer, None, None),
        P(layer, dp, None),
    )
    return jax.shard_map(
        body, mesh=fine, in_specs=in_specs, out_specs=P(layer, dp), check_vma=False
    )
```

```python
import functools
import jax
import jax.numpy as jnp
from jax import lax
from jax.experimental import pallas as pl
from jax.experimental.pallas import tpu as pltpu
from jax.sharding import Mesh, PartitionSpec as P

PIECES = 4


def _own_kernel(copies, x_hbm, c_hbm, n_hbm, pi_hbm, po_hbm, a_hbm, b_hbm, o_ref, x, c, n, pi, po, a, b, sems):
    length, width = x.shape
    rank = pi.shape[0]
    step = width // PIECES
    started = []
    for p in range(PIECES):
        cols = pl.ds(p * step, step)
        group = [
            pltpu.make_async_copy(src.at[:, cols], dst.at[:, cols], sems.at[4 * p + i])
            for i, (src, dst) in enumerate(((c_hbm, c), (po_hbm, po), (x_hbm, x), (pi_hbm, pi)))
        ]
        for copy in group:
            copy.start()
        started.append(group)
    factors = [
        pltpu.make_async_copy(a_hbm, a, sems.at[4 * PIECES]),
        pltpu.make_async_copy(b_hbm, b, sems.at[4 * PIECES + 1]),
        pltpu.make_async_copy(n_hbm, n, sems.at[4 * PIECES + 2]),
    ]
    for copy in factors:
        copy.start()
    out_side = jnp.zeros((rank, length), jnp.float32)
    in_side = jnp.zeros((length, rank), jnp.float32)
    nt = (((1,), (1,)), ((), ()))
    for p in range(PIECES):
        cols = pl.ds(p * step, step)
        group = started[p]
        group[0].wait()
        group[1].wait()
        out_side += lax.dot_general(po[:, cols], c[:, cols], nt, preferred_element_type=jnp.float32)
        group[2].wait()
        group[3].wait()
        in_side += lax.dot_general(x[:, cols], pi[:, cols], nt, preferred_element_type=jnp.float32)
    for copy in factors:
        copy.wait()
    slots = lax.broadcasted_iota(jnp.int32, (rank, length), 1)
    out_side = jnp.where(slots < n[0], out_side, 0.0).astype(jnp.bfloat16)
    grad = jnp.dot(out_side, in_side.astype(jnp.bfloat16), preferred_element_type=jnp.float32)
    grad = grad.astype(jnp.bfloat16).astype(jnp.float32)
    half = rank // 2
    rows = jnp.concatenate([a[pl.ds(0, half, stride=2), :], a[pl.ds(1, half, stride=2), :]], axis=0)
    left = jnp.dot(rows, grad, precision=lax.Precision.HIGHEST, preferred_element_type=jnp.float32)
    both = jnp.dot(left, b[...], precision=lax.Precision.HIGHEST, preferred_element_type=jnp.float32)
    paired = jnp.concatenate([both[:half], both[half:]], axis=1).astype(jnp.bfloat16)
    for i in range(copies):
        o_ref[i] = paired


def own_gradient(copies, x, c, n, pi, po, a, b):
    length, width = x.shape
    rank = pi.shape[0]
    any_ = pl.BlockSpec(memory_space=pl.ANY)
    return pl.pallas_call(
        functools.partial(_own_kernel, copies),
        out_shape=jax.ShapeDtypeStruct((copies, rank // 2, 2 * rank), jnp.bfloat16),
        in_specs=[any_, any_, pl.BlockSpec(memory_space=pltpu.HBM)] + [any_] * 4,
        out_specs=pl.BlockSpec(memory_space=pltpu.VMEM),
        scratch_shapes=[
            pltpu.VMEM((length, width), jnp.bfloat16),
            pltpu.VMEM((length, width), jnp.bfloat16),
            pltpu.SMEM((1,), jnp.int32),
            pltpu.VMEM((rank, width), jnp.bfloat16),
            pltpu.VMEM((rank, width), jnp.bfloat16),
            pltpu.VMEM((rank, rank), jnp.float32),
            pltpu.VMEM((rank, rank), jnp.float32),
            pltpu.SemaphoreType.DMA((4 * PIECES + 3,)),
        ],
        compiler_params=pltpu.CompilerParams(vmem_limit_bytes=16 * 1024 * 1024),
        name="own_gradient",
    )(x, c, n, pi, po, a, b)


CORES = 2
Y_HI = 2
Y_LO = 2
RUN = 4
EARLY = 7


def runs_of(places):
    half = places // RUN // 2
    return [half, *range(half), *range(half + 1, 2 * half)]


def pairs(planes, places):
    over_y = [(h * places + z, (1 - h) * places + z) for z in planes for h in range(Y_HI)]
    over_core = [(CORES * z + c, CORES * z + 1 - c) for z in planes for c in range(CORES)]
    return over_y, over_core


def last_first(count):
    return [[(i + count - 1) % count for i in range(count)]]


def own_sent(query_inputs, query_cotangents, query_lengths, proj_in, proj_out, out_factor, in_factor):
    return own_gradient(
        lax.axis_size("z"),
        pltpu.with_memory_space_constraint(query_inputs[0, 0], pltpu.HBM),
        pltpu.with_memory_space_constraint(query_cotangents[0, 0], pltpu.HBM),
        query_lengths,
        pltpu.with_memory_space_constraint(proj_in[0], pltpu.HBM),
        pltpu.with_memory_space_constraint(proj_out[0], pltpu.HBM),
        pltpu.with_memory_space_constraint(out_factor[0], pltpu.HBM),
        pltpu.with_memory_space_constraint(in_factor[0], pltpu.HBM),
    )


def gathered(sent):
    places = lax.axis_size("z")
    order = [r * RUN + i for r in runs_of(places) for i in range(RUN)]
    return lax.all_to_all(sent, "z", 0, 0, axis_index_groups=[order])


def _mine_kernel(q_ref, core_q_ref, yh_q_ref, mine_ref, o_ref):
    nt = (((1,), (1,)), ((), ()))
    z = lax.axis_index("z")

    def score(more_ref):
        q = jnp.concatenate([q_ref[...], more_ref[...]], axis=0)
        o_ref[...] = lax.dot_general(q, mine_ref[...], nt, preferred_element_type=jnp.float32)

    @pl.when(z < EARLY)
    def _():
        score(core_q_ref)

    @pl.when(z >= EARLY)
    def _():
        score(yh_q_ref)


def scored_mine(*operands):
    vmem = pl.BlockSpec(memory_space=pltpu.VMEM)
    rows, train = 2 * operands[0].shape[0], operands[3].shape[0]
    return pl.pallas_call(
        _mine_kernel,
        out_shape=jax.ShapeDtypeStruct((rows, train), jnp.float32),
        in_specs=[vmem] * 4,
        out_specs=vmem,
        compiler_params=pltpu.CompilerParams(vmem_limit_bytes=16 * 1024 * 1024),
        cost_estimate=pl.CostEstimate(flops=10000000000, bytes_accessed=1 << 20, transcendentals=0),
        name="scored_mine",
    )(*operands)


def _score_kernel(places, q_ref, core_q_ref, yh_q_ref, mine_s, yh_ref, core_ref, o_ref, other_s):
    nt = (((1,), (1,)), ((), ()))
    yh, core, z = lax.axis_index("yh"), lax.axis_index("core"), lax.axis_index("z")
    blocks = o_ref.shape[0]
    layers = blocks // (Y_HI * CORES)
    runs = runs_of(places)
    o_ref[...] = jnp.zeros(o_ref.shape, o_ref.dtype)

    def score(more_ref, other_ref):
        q = jnp.concatenate([q_ref[...], more_ref[...]], axis=0)
        other_s[...] = lax.dot_general(q, other_ref[...], nt, preferred_element_type=jnp.float32)

    def put(h, c, layer, first, second):
        rows = jnp.concatenate([first, second], axis=0).astype(o_ref.dtype)
        o_ref[lax.rem((h * CORES + c) * layers + layer + 1, blocks)] = rows

    @pl.when(z < EARLY)
    def _():
        score(core_q_ref, yh_ref)
        for s, h in ((mine_s, yh), (other_s, 1 - yh)):
            for i, r in enumerate(runs):
                own = s[i * RUN : (i + 1) * RUN]
                more = s[places + i * RUN : places + (i + 1) * RUN]
                first = jnp.where(core == 0, own, more)
                put(h, core, yh * len(runs) + r, first, jnp.where(core == 0, more, own))

    @pl.when(z >= EARLY)
    def _():
        score(yh_q_ref, core_ref)
        for s, c in ((mine_s, core), (other_s, 1 - core)):
            for half, h in ((0, yh), (1, 1 - yh)):
                for i, r in enumerate(runs):
                    at = half * places + i * RUN
                    own = s[at : at + RUN]
                    none = jnp.zeros_like(own)
                    put(yh, c, h * len(runs) + r, jnp.where(core == 0, own, none), jnp.where(core == 0, none, own))


def scored(places, layers, *operands):
    train = operands[3].shape[1]
    vmem = pl.BlockSpec(memory_space=pltpu.VMEM)
    return pl.pallas_call(
        functools.partial(_score_kernel, places),
        out_shape=jax.ShapeDtypeStruct((Y_HI * CORES * layers, CORES * RUN, train), jnp.bfloat16),
        in_specs=[vmem] * 6,
        out_specs=vmem,
        scratch_shapes=[pltpu.VMEM((2 * places, train), jnp.float32)],
        compiler_params=pltpu.CompilerParams(vmem_limit_bytes=16 * 1024 * 1024),
        name="scored",
    )(*operands)


def body(
    query_inputs,
    query_cotangents,
    query_lengths,
    proj_in,
    proj_out,
    out_factor,
    in_factor,
    train_grads,
):
    flat = train_grads.shape[2]
    train = train_grads.shape[1]
    places = lax.axis_size("z")
    layers = lax.axis_size(("x", "yl"))
    mine = train_grads[0]
    early_yh, early_core = pairs(range(EARLY), places)
    late_yh, late_core = pairs(range(EARLY, places), places)
    sent = own_sent(
        query_inputs, query_cotangents, query_lengths, proj_in, proj_out, out_factor, in_factor
    )
    yh_rows = lax.ppermute(mine, ("yh", "z"), early_yh)
    held, yh_rows, after = lax.optimization_barrier((gathered(sent), yh_rows, mine))
    yh_queries = lax.ppermute(held, ("yh", "z"), late_yh)
    core_queries = lax.ppermute(held, ("z", "core"), early_core)
    core_rows = lax.ppermute(after, ("z", "core"), late_core)
    queries = [q.reshape(places, flat) for q in (held, core_queries, yh_queries)]
    parts = scored(places, layers, *queries, scored_mine(*queries, mine), yh_rows, core_rows)
    terms = lax.all_to_all(
        parts, ("yh", "core", "x", "yl"), 0, 0, axis_index_groups=last_first(parts.shape[0])
    )
    terms = jnp.sum(terms.astype(jnp.float32), axis=0)
    return terms.reshape(CORES, RUN, train).transpose(1, 0, 2).reshape(-1, train)


def solution(mesh):
    dp, layer = mesh.devices.shape
    shape = (Y_HI, dp // (Y_HI * CORES), CORES, layer // Y_LO, Y_LO)
    fine = Mesh(mesh.devices.reshape(shape), ("yh", "z", "core", "x", "yl"))
    dp, layer = ("yh", "z", "core"), ("x", "yl")
    in_specs = (
        P(layer, dp, None, None),
        P(layer, dp, None, None),
        P(dp),
        P(layer, None, None),
        P(layer, None, None),
        P(layer, None, None),
        P(layer, None, None),
        P(layer, dp, None),
    )
    return jax.shard_map(
        body, mesh=fine, in_specs=in_specs, out_specs=P(layer, dp), check_vma=False
    )
```

```python
import functools
import jax
import jax.numpy as jnp
from jax import lax
from jax.experimental import pallas as pl
from jax.experimental.pallas import tpu as pltpu
from jax.sharding import Mesh, PartitionSpec as P

PIECES = 4


def _own_kernel(copies, x_hbm, c_hbm, n_hbm, pi_hbm, po_hbm, a_hbm, b_hbm, o_ref, x, c, n, pi, po, a, b, sems):
    length, width = x.shape
    rank = pi.shape[0]
    step = width // PIECES
    started = []
    for p in range(PIECES):
        cols = pl.ds(p * step, step)
        group = [
            pltpu.make_async_copy(src.at[:, cols], dst.at[:, cols], sems.at[4 * p + i])
            for i, (src, dst) in enumerate(((c_hbm, c), (po_hbm, po), (x_hbm, x), (pi_hbm, pi)))
        ]
        for copy in group:
            copy.start()
        started.append(group)
    factors = [
        pltpu.make_async_copy(a_hbm, a, sems.at[4 * PIECES]),
        pltpu.make_async_copy(b_hbm, b, sems.at[4 * PIECES + 1]),
        pltpu.make_async_copy(n_hbm, n, sems.at[4 * PIECES + 2]),
    ]
    for copy in factors:
        copy.start()
    out_side = jnp.zeros((rank, length), jnp.float32)
    in_side = jnp.zeros((length, rank), jnp.float32)
    nt = (((1,), (1,)), ((), ()))
    for p in range(PIECES):
        cols = pl.ds(p * step, step)
        group = started[p]
        group[0].wait()
        group[1].wait()
        out_side += lax.dot_general(po[:, cols], c[:, cols], nt, preferred_element_type=jnp.float32)
        group[2].wait()
        group[3].wait()
        in_side += lax.dot_general(x[:, cols], pi[:, cols], nt, preferred_element_type=jnp.float32)
    for copy in factors:
        copy.wait()
    slots = lax.broadcasted_iota(jnp.int32, (rank, length), 1)
    out_side = jnp.where(slots < n[0], out_side, 0.0).astype(jnp.bfloat16)
    grad = jnp.dot(out_side, in_side.astype(jnp.bfloat16), preferred_element_type=jnp.float32)
    grad = grad.astype(jnp.bfloat16).astype(jnp.float32)
    half = rank // 2
    rows = jnp.concatenate([a[pl.ds(0, half, stride=2), :], a[pl.ds(1, half, stride=2), :]], axis=0)
    left = jnp.dot(rows, grad, precision=lax.Precision.HIGHEST, preferred_element_type=jnp.float32)
    both = jnp.dot(left, b[...], precision=lax.Precision.HIGHEST, preferred_element_type=jnp.float32)
    paired = jnp.concatenate([both[:half], both[half:]], axis=1).astype(jnp.bfloat16)
    for i in range(copies):
        o_ref[i] = paired


def own_gradient(copies, x, c, n, pi, po, a, b):
    length, width = x.shape
    rank = pi.shape[0]
    any_ = pl.BlockSpec(memory_space=pl.ANY)
    return pl.pallas_call(
        functools.partial(_own_kernel, copies),
        out_shape=jax.ShapeDtypeStruct((copies, rank // 2, 2 * rank), jnp.bfloat16),
        in_specs=[any_, any_, pl.BlockSpec(memory_space=pltpu.HBM)] + [any_] * 4,
        out_specs=pl.BlockSpec(memory_space=pltpu.VMEM),
        scratch_shapes=[
            pltpu.VMEM((length, width), jnp.bfloat16),
            pltpu.VMEM((length, width), jnp.bfloat16),
            pltpu.SMEM((1,), jnp.int32),
            pltpu.VMEM((rank, width), jnp.bfloat16),
            pltpu.VMEM((rank, width), jnp.bfloat16),
            pltpu.VMEM((rank, rank), jnp.float32),
            pltpu.VMEM((rank, rank), jnp.float32),
            pltpu.SemaphoreType.DMA((4 * PIECES + 3,)),
        ],
        compiler_params=pltpu.CompilerParams(vmem_limit_bytes=16 * 1024 * 1024),
        name="own_gradient",
    )(x, c, n, pi, po, a, b)


CORES = 2
Y_HI = 2
Y_LO = 2
RUN = 4
EARLY = 7


def order_of(places):
    half = places // 2
    near, far = list(range(RUN)), list(range(half + 1, half + RUN))
    return [half, *near, *far, *range(RUN, half), *range(half + RUN, places)]


def run_at(rows, first, layer, places):
    order = order_of(places)
    at = [first + order.index(layer * RUN + i) for i in range(RUN)]
    return jnp.concatenate([rows[a : a + 1] for a in at], axis=0)


def pairs(planes, places):
    over_y = [(h * places + z, (1 - h) * places + z) for z in planes for h in range(Y_HI)]
    over_core = [(CORES * z + c, CORES * z + 1 - c) for z in planes for c in range(CORES)]
    return over_y, over_core


def last_first(count):
    return [[(i + count - 1) % count for i in range(count)]]


def own_sent(query_inputs, query_cotangents, query_lengths, proj_in, proj_out, out_factor, in_factor):
    return own_gradient(
        lax.axis_size("z"),
        pltpu.with_memory_space_constraint(query_inputs[0, 0], pltpu.HBM),
        pltpu.with_memory_space_constraint(query_cotangents[0, 0], pltpu.HBM),
        query_lengths,
        pltpu.with_memory_space_constraint(proj_in[0], pltpu.HBM),
        pltpu.with_memory_space_constraint(proj_out[0], pltpu.HBM),
        pltpu.with_memory_space_constraint(out_factor[0], pltpu.HBM),
        pltpu.with_memory_space_constraint(in_factor[0], pltpu.HBM),
    )


def gathered(sent):
    places = lax.axis_size("z")
    order = order_of(places)
    return lax.all_to_all(sent, "z", 0, 0, axis_index_groups=[order])


def _mine_kernel(q_ref, core_q_ref, yh_q_ref, mine_ref, o_ref):
    nt = (((1,), (1,)), ((), ()))
    z = lax.axis_index("z")

    def score(more_ref):
        q = jnp.concatenate([q_ref[...], more_ref[...]], axis=0)
        o_ref[...] = lax.dot_general(q, mine_ref[...], nt, preferred_element_type=jnp.float32)

    @pl.when(z < EARLY)
    def _():
        score(core_q_ref)

    @pl.when(z >= EARLY)
    def _():
        score(yh_q_ref)


def scored_mine(*operands):
    vmem = pl.BlockSpec(memory_space=pltpu.VMEM)
    rows, train = 2 * operands[0].shape[0], operands[3].shape[0]
    return pl.pallas_call(
        _mine_kernel,
        out_shape=jax.ShapeDtypeStruct((rows, train), jnp.float32),
        in_specs=[vmem] * 4,
        out_specs=vmem,
        compiler_params=pltpu.CompilerParams(vmem_limit_bytes=16 * 1024 * 1024),
        cost_estimate=pl.CostEstimate(flops=10000000000, bytes_accessed=1 << 20, transcendentals=0),
        name="scored_mine",
    )(*operands)


def _score_kernel(places, q_ref, core_q_ref, yh_q_ref, mine_s, yh_ref, core_ref, o_ref, other_s):
    nt = (((1,), (1,)), ((), ()))
    yh, core, z = lax.axis_index("yh"), lax.axis_index("core"), lax.axis_index("z")
    blocks = o_ref.shape[0]
    layers = blocks // (Y_HI * CORES)
    runs = places // RUN
    o_ref[...] = jnp.zeros(o_ref.shape, o_ref.dtype)

    def score(more_ref, other_ref):
        q = jnp.concatenate([q_ref[...], more_ref[...]], axis=0)
        other_s[...] = lax.dot_general(q, other_ref[...], nt, preferred_element_type=jnp.float32)

    def put(h, c, layer, first, second):
        rows = jnp.concatenate([first, second], axis=0).astype(o_ref.dtype)
        o_ref[lax.rem((h * CORES + c) * layers + layer + 1, blocks)] = rows

    @pl.when(z < EARLY)
    def _():
        score(core_q_ref, yh_ref)
        for s, h in ((mine_s, yh), (other_s, 1 - yh)):
            for r in range(runs):
                own, more = (run_at(s[...], first, r, places) for first in (0, places))
                first = jnp.where(core == 0, own, more)
                put(h, core, yh * runs + r, first, jnp.where(core == 0, more, own))

    @pl.when(z >= EARLY)
    def _():
        score(yh_q_ref, core_ref)
        for s, c in ((mine_s, core), (other_s, 1 - core)):
            for half, h in ((0, yh), (1, 1 - yh)):
                for r in range(runs):
                    own = run_at(s[...], half * places, r, places)
                    none = jnp.zeros_like(own)
                    put(yh, c, h * runs + r, jnp.where(core == 0, own, none), jnp.where(core == 0, none, own))


def scored(places, layers, *operands):
    train = operands[3].shape[1]
    vmem = pl.BlockSpec(memory_space=pltpu.VMEM)
    return pl.pallas_call(
        functools.partial(_score_kernel, places),
        out_shape=jax.ShapeDtypeStruct((Y_HI * CORES * layers, CORES * RUN, train), jnp.bfloat16),
        in_specs=[vmem] * 6,
        out_specs=vmem,
        scratch_shapes=[pltpu.VMEM((2 * places, train), jnp.float32)],
        compiler_params=pltpu.CompilerParams(vmem_limit_bytes=16 * 1024 * 1024),
        name="scored",
    )(*operands)


def body(
    query_inputs,
    query_cotangents,
    query_lengths,
    proj_in,
    proj_out,
    out_factor,
    in_factor,
    train_grads,
):
    flat = train_grads.shape[2]
    train = train_grads.shape[1]
    places = lax.axis_size("z")
    layers = lax.axis_size(("x", "yl"))
    mine = train_grads[0]
    early_yh, early_core = pairs(range(EARLY), places)
    late_yh, late_core = pairs(range(EARLY, places), places)
    sent = own_sent(
        query_inputs, query_cotangents, query_lengths, proj_in, proj_out, out_factor, in_factor
    )
    yh_rows = lax.ppermute(mine, ("yh", "z"), early_yh)
    held, yh_rows, after = lax.optimization_barrier((gathered(sent), yh_rows, mine))
    yh_queries = lax.ppermute(held, ("yh", "z"), late_yh)
    core_queries = lax.ppermute(held, ("z", "core"), early_core)
    core_rows = lax.ppermute(after, ("z", "core"), late_core)
    queries = [q.reshape(places, flat) for q in (held, core_queries, yh_queries)]
    parts = scored(places, layers, *queries, scored_mine(*queries, mine), yh_rows, core_rows)
    terms = lax.all_to_all(
        parts, ("yh", "core", "x", "yl"), 0, 0, axis_index_groups=last_first(parts.shape[0])
    )
    terms = jnp.sum(terms.astype(jnp.float32), axis=0)
    return terms.reshape(CORES, RUN, train).transpose(1, 0, 2).reshape(-1, train)


def solution(mesh):
    dp, layer = mesh.devices.shape
    shape = (Y_HI, dp // (Y_HI * CORES), CORES, layer // Y_LO, Y_LO)
    fine = Mesh(mesh.devices.reshape(shape), ("yh", "z", "core", "x", "yl"))
    dp, layer = ("yh", "z", "core"), ("x", "yl")
    in_specs = (
        P(layer, dp, None, None),
        P(layer, dp, None, None),
        P(dp),
        P(layer, None, None),
        P(layer, None, None),
        P(layer, None, None),
        P(layer, None, None),
        P(layer, dp, None),
    )
    return jax.shard_map(
        body, mesh=fine, in_specs=in_specs, out_specs=P(layer, dp), check_vma=False
    )
```

```python
import functools
import jax
import jax.numpy as jnp
from jax import lax
from jax.experimental import pallas as pl
from jax.experimental.pallas import tpu as pltpu
from jax.sharding import Mesh, PartitionSpec as P

PIECES = 4


def _own_kernel(copies, x_hbm, c_hbm, n_hbm, pi_hbm, po_hbm, a_hbm, b_hbm, o_ref, x, c, n, pi, po, a, b, sems):
    length, width = x.shape
    rank = pi.shape[0]
    step = width // PIECES
    started = []
    for p in range(PIECES):
        cols = pl.ds(p * step, step)
        group = [
            pltpu.make_async_copy(src.at[:, cols], dst.at[:, cols], sems.at[4 * p + i])
            for i, (src, dst) in enumerate(((c_hbm, c), (po_hbm, po), (x_hbm, x), (pi_hbm, pi)))
        ]
        for copy in group:
            copy.start()
        started.append(group)
    factors = [
        pltpu.make_async_copy(a_hbm, a, sems.at[4 * PIECES]),
        pltpu.make_async_copy(b_hbm, b, sems.at[4 * PIECES + 1]),
        pltpu.make_async_copy(n_hbm, n, sems.at[4 * PIECES + 2]),
    ]
    for copy in factors:
        copy.start()
    out_side = jnp.zeros((rank, length), jnp.float32)
    in_side = jnp.zeros((length, rank), jnp.float32)
    nt = (((1,), (1,)), ((), ()))
    for p in range(PIECES):
        cols = pl.ds(p * step, step)
        group = started[p]
        group[0].wait()
        group[1].wait()
        out_side += lax.dot_general(po[:, cols], c[:, cols], nt, preferred_element_type=jnp.float32)
        group[2].wait()
        group[3].wait()
        in_side += lax.dot_general(x[:, cols], pi[:, cols], nt, preferred_element_type=jnp.float32)
    for copy in factors:
        copy.wait()
    slots = lax.broadcasted_iota(jnp.int32, (rank, length), 1)
    out_side = jnp.where(slots < n[0], out_side, 0.0).astype(jnp.bfloat16)
    grad = jnp.dot(out_side, in_side.astype(jnp.bfloat16), preferred_element_type=jnp.float32)
    grad = grad.astype(jnp.bfloat16).astype(jnp.float32)
    half = rank // 2
    rows = jnp.concatenate([a[pl.ds(0, half, stride=2), :], a[pl.ds(1, half, stride=2), :]], axis=0)
    left = jnp.dot(rows, grad, precision=lax.Precision.HIGHEST, preferred_element_type=jnp.float32)
    both = jnp.dot(left, b[...], precision=lax.Precision.HIGHEST, preferred_element_type=jnp.float32)
    paired = jnp.concatenate([both[:half], both[half:]], axis=1).astype(jnp.bfloat16)
    for i in range(copies):
        o_ref[i] = paired


def own_gradient(copies, x, c, n, pi, po, a, b):
    length, width = x.shape
    rank = pi.shape[0]
    any_ = pl.BlockSpec(memory_space=pl.ANY)
    return pl.pallas_call(
        functools.partial(_own_kernel, copies),
        out_shape=jax.ShapeDtypeStruct((copies, rank // 2, 2 * rank), jnp.bfloat16),
        in_specs=[any_, any_, pl.BlockSpec(memory_space=pltpu.HBM)] + [any_] * 4,
        out_specs=pl.BlockSpec(memory_space=pltpu.VMEM),
        scratch_shapes=[
            pltpu.VMEM((length, width), jnp.bfloat16),
            pltpu.VMEM((length, width), jnp.bfloat16),
            pltpu.SMEM((1,), jnp.int32),
            pltpu.VMEM((rank, width), jnp.bfloat16),
            pltpu.VMEM((rank, width), jnp.bfloat16),
            pltpu.VMEM((rank, rank), jnp.float32),
            pltpu.VMEM((rank, rank), jnp.float32),
            pltpu.SemaphoreType.DMA((4 * PIECES + 3,)),
        ],
        compiler_params=pltpu.CompilerParams(vmem_limit_bytes=16 * 1024 * 1024),
        name="own_gradient",
    )(x, c, n, pi, po, a, b)


CORES = 2
Y_HI = 2
Y_LO = 2
RUN = 4
EARLY = 7


def runs_of(places):
    half = places // RUN // 2
    return [r for i in range(half) for r in (half + i, i)]


def pairs(planes, places):
    over_y = [(h * places + z, (1 - h) * places + z) for z in planes for h in range(Y_HI)]
    over_core = [(CORES * z + c, CORES * z + 1 - c) for z in planes for c in range(CORES)]
    return over_y, over_core


def last_first(count):
    return [[(i + count - 1) % count for i in range(count)]]


def own_sent(query_inputs, query_cotangents, query_lengths, proj_in, proj_out, out_factor, in_factor):
    return own_gradient(
        lax.axis_size("z"),
        pltpu.with_memory_space_constraint(query_inputs[0, 0], pltpu.HBM),
        pltpu.with_memory_space_constraint(query_cotangents[0, 0], pltpu.HBM),
        query_lengths,
        pltpu.with_memory_space_constraint(proj_in[0], pltpu.HBM),
        pltpu.with_memory_space_constraint(proj_out[0], pltpu.HBM),
        pltpu.with_memory_space_constraint(out_factor[0], pltpu.HBM),
        pltpu.with_memory_space_constraint(in_factor[0], pltpu.HBM),
    )


def gathered(sent):
    places = lax.axis_size("z")
    order = [r * RUN + i for r in runs_of(places) for i in range(RUN)]
    return lax.all_to_all(sent, "z", 0, 0, axis_index_groups=[order])


def _mine_kernel(q_ref, core_q_ref, yh_q_ref, mine_ref, o_ref):
    nt = (((1,), (1,)), ((), ()))
    z = lax.axis_index("z")

    def score(more_ref):
        q = jnp.concatenate([q_ref[...], more_ref[...]], axis=0)
        o_ref[...] = lax.dot_general(q, mine_ref[...], nt, preferred_element_type=jnp.float32)

    @pl.when(z < EARLY)
    def _():
        score(core_q_ref)

    @pl.when(z >= EARLY)
    def _():
        score(yh_q_ref)


def scored_mine(*operands):
    vmem = pl.BlockSpec(memory_space=pltpu.VMEM)
    rows, train = 2 * operands[0].shape[0], operands[3].shape[0]
    return pl.pallas_call(
        _mine_kernel,
        out_shape=jax.ShapeDtypeStruct((rows, train), jnp.float32),
        in_specs=[vmem] * 4,
        out_specs=vmem,
        compiler_params=pltpu.CompilerParams(vmem_limit_bytes=16 * 1024 * 1024),
        cost_estimate=pl.CostEstimate(flops=10000000000, bytes_accessed=1 << 20, transcendentals=0),
        name="scored_mine",
    )(*operands)


def _score_kernel(places, q_ref, core_q_ref, yh_q_ref, mine_s, yh_ref, core_ref, o_ref, other_s):
    nt = (((1,), (1,)), ((), ()))
    yh, core, z = lax.axis_index("yh"), lax.axis_index("core"), lax.axis_index("z")
    blocks = o_ref.shape[0]
    layers = blocks // (Y_HI * CORES)
    runs = runs_of(places)
    o_ref[...] = jnp.zeros(o_ref.shape, o_ref.dtype)

    def score(more_ref, other_ref):
        q = jnp.concatenate([q_ref[...], more_ref[...]], axis=0)
        other_s[...] = lax.dot_general(q, other_ref[...], nt, preferred_element_type=jnp.float32)

    def put(h, c, layer, first, second):
        rows = jnp.concatenate([first, second], axis=0).astype(o_ref.dtype)
        o_ref[lax.rem((h * CORES + c) * layers + layer + 1, blocks)] = rows

    @pl.when(z < EARLY)
    def _():
        score(core_q_ref, yh_ref)
        for s, h in ((mine_s, yh), (other_s, 1 - yh)):
            for i, r in enumerate(runs):
                own = s[i * RUN : (i + 1) * RUN]
                more = s[places + i * RUN : places + (i + 1) * RUN]
                first = jnp.where(core == 0, own, more)
                put(h, core, yh * len(runs) + r, first, jnp.where(core == 0, more, own))

    @pl.when(z >= EARLY)
    def _():
        score(yh_q_ref, core_ref)
        for s, c in ((mine_s, core), (other_s, 1 - core)):
            for half, h in ((0, yh), (1, 1 - yh)):
                for i, r in enumerate(runs):
                    at = half * places + i * RUN
                    own = s[at : at + RUN]
                    none = jnp.zeros_like(own)
                    put(yh, c, h * len(runs) + r, jnp.where(core == 0, own, none), jnp.where(core == 0, none, own))


def scored(places, layers, *operands):
    train = operands[3].shape[1]
    vmem = pl.BlockSpec(memory_space=pltpu.VMEM)
    return pl.pallas_call(
        functools.partial(_score_kernel, places),
        out_shape=jax.ShapeDtypeStruct((Y_HI * CORES * layers, CORES * RUN, train), jnp.bfloat16),
        in_specs=[vmem] * 6,
        out_specs=vmem,
        scratch_shapes=[pltpu.VMEM((2 * places, train), jnp.float32)],
        compiler_params=pltpu.CompilerParams(vmem_limit_bytes=16 * 1024 * 1024),
        name="scored",
    )(*operands)


def body(
    query_inputs,
    query_cotangents,
    query_lengths,
    proj_in,
    proj_out,
    out_factor,
    in_factor,
    train_grads,
):
    flat = train_grads.shape[2]
    train = train_grads.shape[1]
    places = lax.axis_size("z")
    layers = lax.axis_size(("x", "yl"))
    mine = train_grads[0]
    early_yh, early_core = pairs(range(EARLY), places)
    late_yh, late_core = pairs(range(EARLY, places), places)
    sent = own_sent(
        query_inputs, query_cotangents, query_lengths, proj_in, proj_out, out_factor, in_factor
    )
    yh_rows = lax.ppermute(mine, ("yh", "z"), early_yh)
    held, yh_rows, after = lax.optimization_barrier((gathered(sent), yh_rows, mine))
    yh_queries = lax.ppermute(held, ("yh", "z"), late_yh)
    core_queries = lax.ppermute(held, ("z", "core"), early_core)
    core_rows = lax.ppermute(after, ("z", "core"), late_core)
    queries = [q.reshape(places, flat) for q in (held, core_queries, yh_queries)]
    parts = scored(places, layers, *queries, scored_mine(*queries, mine), yh_rows, core_rows)
    terms = lax.all_to_all(
        parts, ("yh", "core", "x", "yl"), 0, 0, axis_index_groups=last_first(parts.shape[0])
    )
    terms = jnp.sum(terms.astype(jnp.float32), axis=0)
    return terms.reshape(CORES, RUN, train).transpose(1, 0, 2).reshape(-1, train)


def solution(mesh):
    dp, layer = mesh.devices.shape
    shape = (Y_HI, dp // (Y_HI * CORES), CORES, layer // Y_LO, Y_LO)
    fine = Mesh(mesh.devices.reshape(shape), ("yh", "z", "core", "x", "yl"))
    dp, layer = ("yh", "z", "core"), ("x", "yl")
    in_specs = (
        P(layer, dp, None, None),
        P(layer, dp, None, None),
        P(dp),
        P(layer, None, None),
        P(layer, None, None),
        P(layer, None, None),
        P(layer, None, None),
        P(layer, dp, None),
    )
    return jax.shard_map(
        body, mesh=fine, in_specs=in_specs, out_specs=P(layer, dp), check_vma=False
    )
```
